128 devices in a mesh: dp: 8 (over x, z_lo), tensor: 16 (over y, z_hi, core).
Axes of the slice: x: 4, y: 4, z: 4 (z_hi: 2, z_lo: 2; z = z_hi * 2 + z_lo), core: 2. Of those that a mesh axis runs over, the one named last changes fastest.
Arguments:
- gate_pre: bfloat16 [1024, 65536], P('dp', 'tensor'), may hold values from -6 to 6
- up_pre: bfloat16 [1024, 65536], P('dp', 'tensor'), may hold values from -6 to 6
- down_weight: bfloat16 [65536, 16384], P('tensor', 'dp'), may hold values from -0.0234375 to 0.0234375
Outputs:
- mixed: bfloat16 [1024, 16384], P('tensor', 'dp')
The draws below stay inside these ranges and needn't reach their ends.
All inputs are finite; a program needn't handle non-finite values.
Results may differ from the reference program's by a relative error of at most 0.015.
Values may be sent and summed in bfloat16 or wider, within the bound.
A program may use at most 128 MiB of HBM per device.

```python
import jax
import jax.numpy as jnp

D = 16384
FF = 65536
TOKENS = 1024


def block_levels(rng, shape, cuts, low, high):
    gain = 1.0
    for dim, blocks in cuts:
        heights = jax.random.uniform(jax.random.fold_in(jax.random.fold_in(rng, 6), dim), (blocks,), jnp.float32, low / len(cuts), high / len(cuts))
        gain = gain * jnp.repeat(jnp.exp(heights), shape[dim] // blocks).reshape((-1,) + (1,) * (len(shape) - 1 - dim))
    return gain


def centred(stream_key, extent, scale, most, cuts=(), dtype=jnp.bfloat16):
    gain = block_levels(stream_key, extent, cuts, -0.22, 0.18) if cuts else 1.0
    result = jax.random.normal(stream_key, extent, jnp.float32) * scale * gain
    return jnp.minimum(jnp.maximum(result, -most), most).astype(dtype)


def setup_inputs(seed: int = 0) -> dict:
    seeds = jax.random.split(jax.random.key(seed), 4)
    gate_pre = centred(seeds[0], (TOKENS, FF), 1.0, 6.0, ((0, 8), (1, 16)))
    up_pre = centred(seeds[1], (TOKENS, FF), 1.0, 6.0, ((0, 8), (1, 16)))
    down_weight = centred(seeds[2], (FF, D), FF ** -0.5, 0.0234375, ((0, 16), (1, 8)))
    return dict(gate_pre=gate_pre, up_pre=up_pre, down_weight=down_weight)


def walsh(values):
    rows, width = values.shape
    half = 1
    while half < width:
        shaped = values.reshape(rows, width // (2 * half), 2, half)
        first = shaped[:, :, 0, :]
        second = shaped[:, :, 1, :]
        values = jnp.stack([first + second, first - second], axis=2).reshape(rows, width)
        half = half * 2
    return values


def reference(gate_pre, up_pre, down_weight):
    hidden = (jax.nn.silu(gate_pre.astype(jnp.float32)) * up_pre.astype(jnp.float32)).astype(jnp.bfloat16)
    rotated = walsh(hidden.astype(jnp.float32)) * (1.0 / (FF ** 0.5))
    rotated = rotated.astype(jnp.bfloat16)
    return jnp.dot(rotated, down_weight, preferred_element_type=jnp.float32).astype(jnp.bfloat16)
```

```python
import functools

import jax
import jax.numpy as jnp
import numpy as np
from jax import lax
from jax.experimental import pallas as pl
from jax.experimental.pallas import tpu as pltpu
from jax.sharding import PartitionSpec as P

MESH = pl.DeviceIdType.MESH
INNER = 256
ROWS = 16
TILE = 256


def sylvester(order):
    table = np.ones((1, 1), np.float32)
    while table.shape[0] < order:
        table = np.block([[table, table], [table, -table]])
    return table


def butterfly(parts):
    half = 1
    while half < len(parts):
        for i in range(len(parts)):
            if i // half % 2 == 0:
                first, second = parts[i], parts[i + half]
                parts[i], parts[i + half] = first + second, first - second
        half = half * 2
    return parts


def kernel(
    scale, gate_hbm, up_hbm, weight_hbm, table_ref, out_ref,
    gate, up, weight, mixed, local, arrived, rotated, gathered, theirs, ours, swapped, shares, landed,
    load_sem, weight_sem, send1, recv1, send2, recv2, send3, up3, down3, send4, recv4, send5, recv5, send6, recv6,
):
    dp, tensor = lax.axis_index("dp"), lax.axis_index("tensor")
    groups, blocks = lax.axis_size("tensor"), lax.axis_size("dp")
    chunks = gate.shape[0]
    half = weight.shape[1] // 2
    core, chip = tensor % 2, tensor // 2
    near = dp + 1 - 2 * (dp % 2)
    ahead, behind = (dp + 2) % blocks, (dp + blocks - 2) % blocks
    peers = [(tensor + i) % groups for i in range(groups)]
    pair = 2 * (dp // 2) * ROWS

    def remote(src, dst, send, recv, device):
        pltpu.make_async_remote_copy(
            src_ref=src, dst_ref=dst, send_sem=send, recv_sem=recv, device_id=device, device_id_type=MESH
        ).start()

    def await_bytes(like, sem):
        pltpu.make_async_copy(like, like, sem).wait()

    def first_row(j):
        return pl.multiple_of(j % 2 * (chunks // 2 * ROWS) + j // 2 * ROWS, ROWS)

    for j in range(chunks):
        rows = pl.ds(first_row(j), ROWS)
        pltpu.make_async_copy(gate_hbm.at[rows], gate.at[j], load_sem.at[j]).start()
        pltpu.make_async_copy(up_hbm.at[rows], up.at[j], load_sem.at[j]).start()
    pltpu.make_async_copy(weight_hbm, weight, weight_sem).start()

    barrier = pltpu.get_barrier_semaphore()
    met = [(dp, p) for p in peers[1:]] + [(near, p) for p in peers] + [(ahead, tensor), (behind, tensor)]
    for device in met:
        pl.semaphore_signal(barrier, inc=1, device_id=device, device_id_type=MESH)

    def rotate_local(j):
        await_bytes(gate.at[j], load_sem.at[j])
        await_bytes(up.at[j], load_sem.at[j])
        hidden = []
        for a in range(gate.shape[2] // INNER):
            cols = pl.ds(a * INNER, INNER)
            v = gate[j, :, cols].astype(jnp.float32)
            u = up[j, :, cols].astype(jnp.float32)
            hidden.append((v / (1.0 + jnp.exp(-v)) * u).astype(jnp.bfloat16))
        mixed[...] = jnp.dot(
            jnp.concatenate(hidden, axis=0), table_ref[...], preferred_element_type=jnp.float32
        )
        for lane in range(0, INNER, 128):
            parts = [mixed[pl.ds(a * ROWS, ROWS), pl.ds(lane, 128)] for a in range(len(hidden))]
            for a, part in enumerate(butterfly(parts)):
                local[j, :, pl.ds(a * INNER + lane, 128)] = part.astype(jnp.bfloat16)

    def send_local(j):
        pltpu.make_async_copy(
            local.at[j, :, pl.ds(pl.multiple_of(tensor * INNER, INNER), INNER)],
            arrived.at[j * groups + tensor],
            recv1.at[j],
        ).start()
        for p in peers[1:]:
            remote(
                local.at[j, :, pl.ds(pl.multiple_of(p * INNER, INNER), INNER)],
                arrived.at[j * groups + tensor],
                send1.at[j], recv1.at[j], (dp, p),
            )

    def rotate_groups(j):
        await_bytes(arrived.at[pl.ds(j * groups, groups)], recv1.at[j])
        for lane in range(0, INNER, 128):
            lanes = pl.ds(lane, 128)
            parts = [arrived[j * groups + g, :, lanes].astype(jnp.float32) for g in range(groups)]
            for g, part in enumerate(butterfly(parts)):
                rotated[j * groups + g, :, lanes] = (part * scale).astype(jnp.bfloat16)
        here = gathered.at[
            j,
            pl.ds(pl.multiple_of(dp * ROWS, ROWS), ROWS),
            pl.ds(pl.multiple_of(tensor * INNER, INNER), INNER),
        ]
        pltpu.make_async_copy(rotated.at[j * groups + tensor], here, recv2.at[j]).start()
        for p in peers[1:]:
            remote(rotated.at[j * groups + p], here, send2.at[j], recv2.at[j], (dp, p))
        for p in peers:
            remote(rotated.at[j * groups + p], here, send2.at[j], recv2.at[j], (near, p))

    def send_along(j):
        mine = gathered.at[j, pl.ds(pl.multiple_of(pair, 2 * ROWS), 2 * ROWS)]
        await_bytes(mine, recv2.at[j])
        remote(mine, mine, send3.at[j], up3.at[j], (ahead, tensor))
        remote(mine, mine, send3.at[j], down3.at[j], (behind, tensor))

    def forward(j):
        from_behind = 2 * (behind // 2) * ROWS
        from_ahead = 2 * (ahead // 2) * ROWS
        await_bytes(gathered.at[j, pl.ds(0, 2 * ROWS)], up3.at[j])
        first = gathered.at[j, pl.ds(pl.multiple_of(from_behind, ROWS), ROWS)]
        remote(first, first, send4.at[j], recv4.at[j], (ahead, tensor))
        await_bytes(gathered.at[j, pl.ds(0, 2 * ROWS)], down3.at[j])
        second = gathered.at[j, pl.ds(pl.multiple_of(from_ahead + ROWS, ROWS), ROWS)]
        remote(second, second, send4.at[j], recv4.at[j], (behind, tensor))

    def project(j):
        await_bytes(gathered.at[j, pl.ds(0, 2 * ROWS)], recv4.at[j])

        @pl.loop(0, half // TILE)
        def _(n):
            cols = pl.ds(pl.multiple_of((1 - core) * half + n * TILE, TILE), TILE)
            term = jnp.dot(gathered[j], weight[:, cols], preferred_element_type=jnp.float32)
            theirs[j, :, pl.ds(pl.multiple_of(n * TILE, TILE), TILE)] = term.astype(jnp.bfloat16)

        remote(theirs.at[j], swapped.at[j], send5.at[j], recv5.at[j], (dp, tensor + 1 - 2 * core))

        @pl.loop(0, half // TILE)
        def _(n):
            cols = pl.ds(pl.multiple_of(core * half + n * TILE, TILE), TILE)
            term = jnp.dot(gathered[j], weight[:, cols], preferred_element_type=jnp.float32)
            ours[:, pl.ds(pl.multiple_of(n * TILE, TILE), TILE)] = term

    def scatter(j):
        await_bytes(swapped.at[j], recv5.at[j])
        owner_core = j % 2
        there = landed.at[
            j // 2,
            pl.ds(pl.multiple_of(chip * ROWS, ROWS), ROWS),
            pl.ds(pl.multiple_of(core * half, half), half),
        ]
        for block in range(blocks):
            rows = pl.ds(block * ROWS, ROWS)
            shares[j, rows, :] = (ours[rows, :] + swapped[j, rows, :].astype(jnp.float32)).astype(jnp.bfloat16)
        for i in range(blocks):
            block = (chip + i) % blocks
            owner = block * 2 + owner_core
            share = shares.at[j, pl.ds(pl.multiple_of(block * ROWS, ROWS), ROWS)]
            if i == 0:

                @pl.when(core == owner_core)
                def _():
                    pltpu.make_async_copy(share, there, recv6.at[j // 2]).start()

                @pl.when(core != owner_core)
                def _():
                    remote(share, there, send6.at[j], recv6.at[j // 2], (dp, owner))
            else:
                remote(share, there, send6.at[j], recv6.at[j // 2], (dp, owner))

    def finish(j):
        await_bytes(landed.at[j // 2], recv6.at[j // 2])
        rows = pl.ds(pl.multiple_of(j // 2 * ROWS, ROWS), ROWS)
        for lane in range(0, 2 * half, 512):
            lanes = pl.ds(lane, 512)
            total = landed[j // 2, pl.ds(0, ROWS), lanes].astype(jnp.float32)
            for i in range(1, blocks):
                total = total + landed[j // 2, pl.ds(i * ROWS, ROWS), lanes].astype(jnp.float32)
            out_ref[rows, lanes] = total.astype(jnp.bfloat16)

    rotate_local(0)
    pl.semaphore_wait(barrier, len(met))

    @pl.loop(0, chunks + 6)
    def _(s):
        @pl.when(s < chunks)
        def _():
            @pl.when(s > 0)
            def _():
                rotate_local(s)

            send_local(s)

        @pl.when((s >= 1) & (s < chunks + 1))
        def _():
            rotate_groups(s - 1)

        @pl.when((s >= 2) & (s < chunks + 2))
        def _():
            send_along(s - 2)

        @pl.when((s >= 3) & (s < chunks + 3))
        def _():
            forward(s - 3)

        @pl.when((s >= 5) & (s < chunks + 5))
        def _():
            scatter(s - 5)

        @pl.when(s == 4)
        def _():
            pltpu.make_async_copy(weight_hbm, weight, weight_sem).wait()

        @pl.when((s >= 4) & (s < chunks + 4))
        def _():
            project(s - 4)

        @pl.when((s >= 6) & (s % 2 == core))
        def _():
            finish(s - 6)

    @pl.loop(0, chunks)
    def _(j):
        await_bytes(arrived.at[pl.ds(0, groups - 1)], send1.at[j])
        await_bytes(rotated.at[pl.ds(0, 2 * groups - 1)], send2.at[j])
        await_bytes(gathered.at[j, pl.ds(0, 4 * ROWS)], send3.at[j])
        await_bytes(gathered.at[j, pl.ds(0, 2 * ROWS)], send4.at[j])
        await_bytes(theirs.at[j], send5.at[j])
        await_bytes(shares.at[j, pl.ds(0, (blocks - 1) * ROWS)], send6.at[j])

        @pl.when(core != j % 2)
        def _():
            await_bytes(shares.at[j, pl.ds(0, ROWS)], send6.at[j])


def body(gate_pre, up_pre, down_weight):
    rows, ff_dev = gate_pre.shape
    width = down_weight.shape[1]
    groups, blocks = lax.axis_size("tensor"), lax.axis_size("dp")
    chunks = rows // ROWS
    half = width // 2
    order = ff_dev * groups
    table = jnp.asarray(sylvester(INNER), jnp.bfloat16)
    bf16 = jnp.bfloat16
    dma = pltpu.SemaphoreType.DMA
    return pl.pallas_call(
        functools.partial(kernel, 1.0 / order**0.5),
        out_shape=jax.ShapeDtypeStruct((rows * blocks // groups, width), bf16),
        in_specs=[pl.BlockSpec(memory_space=pl.ANY)] * 3 + [pl.BlockSpec(memory_space=pltpu.VMEM)],
        out_specs=pl.BlockSpec(memory_space=pltpu.VMEM),
        scratch_shapes=[
            pltpu.VMEM((chunks, ROWS, ff_dev), bf16),
            pltpu.VMEM((chunks, ROWS, ff_dev), bf16),
            pltpu.VMEM((ff_dev, width), bf16),
            pltpu.VMEM((ff_dev // INNER * ROWS, INNER), jnp.float32),
            pltpu.VMEM((chunks, ROWS, ff_dev), bf16),
            pltpu.VMEM((chunks * groups, ROWS, INNER), bf16),
            pltpu.VMEM((chunks * groups, ROWS, INNER), bf16),
            pltpu.VMEM((chunks, blocks * ROWS, ff_dev), bf16),
            pltpu.VMEM((chunks, blocks * ROWS, half), bf16),
            pltpu.VMEM((blocks * ROWS, half), jnp.float32),
            pltpu.VMEM((chunks, blocks * ROWS, half), bf16),
            pltpu.VMEM((chunks, blocks * ROWS, half), bf16),
            pltpu.VMEM((chunks // 2, blocks * ROWS, width), bf16),
            dma((chunks,)),
            dma,
        ]
        + [dma((chunks,))] * 11
        + [dma((chunks,)), dma((chunks // 2,))],
        compiler_params=pltpu.CompilerParams(
            collective_id=0, has_side_effects=True, vmem_limit_bytes=56 * 2**20
        ),
        cost_estimate=pl.CostEstimate(
            flops=2 * rows * blocks * ff_dev * width,
            bytes_accessed=2 * ff_dev * width + 4 * rows * ff_dev,
            transcendentals=rows * ff_dev,
        ),
    )(gate_pre, up_pre, down_weight, table)


def solution(mesh):
    placed = (P("dp", "tensor"), P("dp", "tensor"), P("tensor", "dp"))
    return jax.shard_map(
        body, mesh=mesh, in_specs=placed, out_specs=P("tensor", "dp"), check_vma=False
    )
```

```python
import functools

import jax
import jax.numpy as jnp
import numpy as np
from jax import lax
from jax.experimental import pallas as pl
from jax.experimental.pallas import tpu as pltpu
from jax.sharding import PartitionSpec as P

MESH = pl.DeviceIdType.MESH
INNER = 256
ROWS = 16
TILE = 256


def sylvester(order):
    table = np.ones((1, 1), np.float32)
    while table.shape[0] < order:
        table = np.block([[table, table], [table, -table]])
    return table


def butterfly(parts):
    half = 1
    while half < len(parts):
        for i in range(len(parts)):
            if i // half % 2 == 0:
                first, second = parts[i], parts[i + half]
                parts[i], parts[i + half] = first + second, first - second
        half = half * 2
    return parts


def kernel(
    scale, near_until, direct_from, gate_hbm, up_hbm, weight_hbm, table_ref, out_ref,
    gate, up, weight, mixed, local, arrived, rotated, gathered, theirs, ours, swapped, shares, landed, over_y, sums, over_z, result,
    load_sem, weight_sem, out_sem, send1, recv1, send2, recv2_own, recv2_near, send3, up3_own, up3_near, down3_own, down3_near,
    send4, recv4, send5, recv5, send6, recv6, send7, recv7, send8, recv8,
):
    dp, tensor = lax.axis_index("dp"), lax.axis_index("tensor")
    groups, blocks = lax.axis_size("tensor"), lax.axis_size("dp")
    chunks = gate.shape[0]
    half = weight.shape[1] // 2
    width = gate.shape[2]
    core, chip = tensor % 2, tensor // 2
    row, high = chip // 2, chip % 2
    near = dp + 1 - 2 * (dp % 2)
    ahead, behind, opposite = (dp + 2) % blocks, (dp + blocks - 2) % blocks, (dp + 4) % blocks
    peers = [(tensor + i) % groups for i in range(groups)]

    def remote(src, dst, send, recv, device):
        pltpu.make_async_remote_copy(
            src_ref=src, dst_ref=dst, send_sem=send, recv_sem=recv, device_id=device, device_id_type=MESH
        ).start()

    def await_bytes(like, sem):
        pltpu.make_async_copy(like, like, sem).wait()

    def tiles(i, n=1):
        return pl.ds(pl.multiple_of(i * ROWS, ROWS), n * ROWS)

    def first_row(j):
        return pl.multiple_of(j % 2 * (chunks // 2 * ROWS) + j // 2 * ROWS, ROWS)

    barrier = pltpu.get_barrier_semaphore()
    met = [(dp, p) for p in peers[1:]] + [(near, tensor), (ahead, tensor), (behind, tensor)]
    for device in met:
        pl.semaphore_signal(barrier, inc=1, device_id=device, device_id_type=MESH)

    for j in range(chunks):
        rows = pl.ds(first_row(j), ROWS)
        pltpu.make_async_copy(gate_hbm.at[rows], gate.at[j], load_sem.at[j]).start()
        pltpu.make_async_copy(up_hbm.at[rows], up.at[j], load_sem.at[j]).start()
    pltpu.make_async_copy(weight_hbm, weight, weight_sem).start()

    def rotate_local(j):
        await_bytes(gate.at[pl.ds(0, 2)], load_sem.at[j])
        hidden = []
        for a in range(width // INNER):
            cols = pl.ds(a * INNER, INNER)
            v = gate[j, :, cols].astype(jnp.float32)
            u = up[j, :, cols].astype(jnp.float32)
            hidden.append((v / (1.0 + jnp.exp(-v)) * u).astype(jnp.bfloat16))
        mixed[...] = jnp.dot(
            jnp.concatenate(hidden, axis=0), table_ref[...], preferred_element_type=jnp.float32
        )
        for lane in range(0, INNER, 128):
            parts = [mixed[pl.ds(a * ROWS, ROWS), pl.ds(lane, 128)] for a in range(len(hidden))]
            for a, part in enumerate(butterfly(parts)):
                local[j, :, pl.ds(a * INNER + lane, 128)] = part.astype(jnp.bfloat16)

    def piece(i):
        return pl.ds(pl.multiple_of(i * INNER, INNER), INNER)

    def send_local(j):
        slot = arrived.at[j * groups + tensor]
        pltpu.make_async_copy(local.at[j, :, piece(tensor)], slot, recv1.at[j]).start()
        for p in peers[1:]:
            remote(local.at[j, :, piece(p)], slot, send1.at[j], recv1.at[j], (dp, p))

    def rotate_groups(j):
        await_bytes(arrived.at[pl.ds(j * groups, groups)], recv1.at[j])
        for lane in range(0, INNER, 128):
            lanes = pl.ds(lane, 128)
            parts = [arrived[j * groups + g, :, lanes].astype(jnp.float32) for g in range(groups)]
            for g, part in enumerate(butterfly(parts)):
                rotated[j * groups + g, :, lanes] = (part * scale).astype(jnp.bfloat16)
        here = gathered.at[j, tiles(dp), piece(tensor)]
        pltpu.make_async_copy(rotated.at[j * groups + tensor], here, recv2_own.at[j]).start()
        for p in peers[1:]:
            remote(rotated.at[j * groups + p], here, send2.at[j], recv2_own.at[j], (dp, p))
        for p in peers:
            remote(rotated.at[j * groups + p], here, send2.at[j], recv2_near.at[j], (near, p))

    def tile(j, block):
        return gathered.at[j, tiles(block)]

    def left(j, block):
        return gathered.at[j, tiles(block), pl.ds(0, width // 2)]

    def right(j, block):
        return gathered.at[j, tiles(block), pl.ds(width // 2, width // 2)]

    def plane(block):
        return block + 1 - 2 * (dp % 2)

    def send_along(j):
        own, other = tile(j, dp), tile(j, near)

        @pl.when(j < near_until)
        def _():
            await_bytes(own, recv2_own.at[j])
            remote(own, own, send3.at[j], up3_own.at[j], (ahead, tensor))
            remote(own, own, send3.at[j], down3_own.at[j], (behind, tensor))
            await_bytes(other, recv2_near.at[j])
            remote(other, other, send3.at[j], up3_near.at[j], (ahead, tensor))
            remote(other, other, send3.at[j], down3_near.at[j], (behind, tensor))

        @pl.when(j >= near_until)
        def _():
            await_bytes(own, recv2_own.at[j])
            await_bytes(other, recv2_near.at[j])
            remote(own, own, send3.at[j], up3_own.at[j], (ahead, tensor))
            remote(other, other, send3.at[j], down3_near.at[j], (behind, tensor))
            remote(other, other, send3.at[j], up3_near.at[j], (ahead, tensor))
            remote(own, own, send3.at[j], down3_own.at[j], (behind, tensor))

    def forward(j):
        await_bytes(tile(j, behind), up3_own.at[j])

        @pl.when(j < near_until)
        def _():
            first, second = left(j, behind), right(j, ahead)
            remote(first, first, send4.at[j], recv4.at[j], (ahead, tensor))
            await_bytes(tile(j, ahead), down3_own.at[j])
            remote(second, second, send4.at[j], recv4.at[j], (behind, tensor))

        @pl.when(j >= near_until)
        def _():
            first, second = tile(j, behind), tile(j, plane(ahead))
            remote(first, first, send4.at[j], recv4.at[j], (ahead, tensor))
            await_bytes(second, down3_near.at[j])
            remote(second, second, send4.at[j], recv4.at[j], (behind, tensor))

    def across(j):
        @pl.when(j < near_until)
        def _():
            far = tile(j, opposite)
            await_bytes(far, recv4.at[j])
            remote(far, far, send7.at[j], recv7.at[j], (near, tensor))

    def project(j):
        await_bytes(tile(j, plane(behind)), up3_near.at[j])

        @pl.when(j < near_until)
        def _():
            await_bytes(tile(j, plane(ahead)), down3_near.at[j])
            await_bytes(tile(j, plane(opposite)), recv7.at[j])

        @pl.when(j >= near_until)
        def _():
            await_bytes(tile(j, ahead), down3_own.at[j])
            await_bytes(gathered.at[j, pl.ds(0, 2 * ROWS)], recv4.at[j])

        @pl.loop(0, half // TILE)
        def _(n):
            cols = pl.ds(pl.multiple_of((1 - core) * half + n * TILE, TILE), TILE)
            term = jnp.dot(gathered[j], weight[:, cols], preferred_element_type=jnp.float32)
            theirs[j, :, pl.ds(pl.multiple_of(n * TILE, TILE), TILE)] = term.astype(jnp.bfloat16)

        remote(theirs.at[j], swapped.at[j], send5.at[j], recv5.at[j], (dp, tensor + 1 - 2 * core))

        @pl.loop(0, half // TILE)
        def _(n):
            cols = pl.ds(pl.multiple_of(core * half + n * TILE, TILE), TILE)
            term = jnp.dot(gathered[j], weight[:, cols], preferred_element_type=jnp.float32)
            ours[:, pl.ds(pl.multiple_of(n * TILE, TILE), TILE)] = term

    mine = pl.ds(pl.multiple_of(core * half, half), half)

    def deliver(j, share, there, send, recv, owner):
        @pl.when(core == j % 2)
        def _():
            pltpu.make_async_copy(share, there, recv).start()

        @pl.when(core != j % 2)
        def _():
            remote(share, there, send, recv, (dp, owner))

    def scatter(j):
        await_bytes(swapped.at[j], recv5.at[j])
        for block in range(blocks):
            rows = pl.ds(block * ROWS, ROWS)
            shares[j, rows, :] = (ours[rows, :] + swapped[j, rows, :].astype(jnp.float32)).astype(jnp.bfloat16)

        @pl.when(j < direct_from)
        def _():
            slot = over_y.at[j, tiles(2 * row, 2)]
            own = shares.at[j, tiles(2 * row, 2)]
            pltpu.make_async_copy(own, slot, recv6.at[j]).start()
            for i in range(1, 4):
                to = (row + i) % 4
                part = shares.at[j, tiles(2 * to, 2)]
                remote(part, slot, send6.at[j], recv6.at[j], (dp, to * 4 + high * 2 + core))

        @pl.when(j >= direct_from)
        def _():
            there = landed.at[j // 2 - direct_from // 2, tiles(chip), mine]
            deliver(j, shares.at[j, tiles(chip)], there, send6.at[j], recv6.at[j], chip * 2 + j % 2)
            for i in range(1, blocks):
                to = (chip + i) % blocks
                share = shares.at[j, tiles(to)]
                remote(share, there, send6.at[j], recv6.at[j], (dp, to * 2 + j % 2))

    def scatter_z(j):
        @pl.when(j < direct_from)
        def _():
            await_bytes(over_y.at[j], recv6.at[j])
            for part in range(2):
                total = over_y[j, pl.ds(part * ROWS, ROWS), :].astype(jnp.float32)
                for i in range(1, 4):
                    total = total + over_y[j, pl.ds((2 * i + part) * ROWS, ROWS), :].astype(jnp.float32)
                sums[j, pl.ds(part * ROWS, ROWS), :] = total.astype(jnp.bfloat16)
            there = over_z.at[j // 2, tiles(high), mine]
            other = row * 4 + (1 - high) * 2 + j % 2
            remote(sums.at[j, tiles(1 - high)], there, send8.at[j], recv8.at[j], (dp, other))
            deliver(j, sums.at[j, tiles(high)], there, send8.at[j], recv8.at[j], chip * 2 + j % 2)

    def finish(j):
        rows = tiles(j // 2)

        def add(source, count):
            for lane in range(0, 2 * half, 512):
                lanes = pl.ds(lane, 512)
                total = source[pl.ds(0, ROWS), lanes].astype(jnp.float32)
                for i in range(1, count):
                    total = total + source[pl.ds(i * ROWS, ROWS), lanes].astype(jnp.float32)
                result[rows, lanes] = total.astype(jnp.bfloat16)

        @pl.when(j < direct_from)
        def _():
            await_bytes(over_z.at[j // 2], recv8.at[j])
            add(over_z.at[j // 2], 2)

        @pl.when(j >= direct_from)
        def _():
            await_bytes(landed.at[j // 2 - direct_from // 2], recv6.at[j])
            add(landed.at[j // 2 - direct_from // 2], blocks)

        pltpu.make_async_copy(result.at[rows], out_ref.at[rows], out_sem.at[j // 2]).start()

    rotate_local(0)
    pl.semaphore_wait(barrier, len(met))

    @pl.loop(0, chunks + 8)
    def _(s):
        def stage(offset, *steps):
            @pl.when((s >= offset) & (s < chunks + offset))
            def _():
                for step in steps:
                    step(s - offset)

        @pl.when((s >= 1) & (s < chunks))
        def _():
            rotate_local(s)

        stage(0, send_local)
        stage(1, rotate_groups)
        stage(2, send_along)
        stage(3, forward)
        stage(4, across)
        stage(6, scatter)
        stage(7, scatter_z)

        @pl.when(s == 5)
        def _():
            pltpu.make_async_copy(weight_hbm, weight, weight_sem).wait()

        stage(5, project)

        @pl.when((s >= 8) & (s % 2 == core))
        def _():
            finish(s - 8)

    @pl.loop(0, chunks)
    def _(j):
        await_bytes(arrived.at[pl.ds(0, groups - 1)], send1.at[j])
        await_bytes(rotated.at[pl.ds(0, 2 * groups - 1)], send2.at[j])
        await_bytes(gathered.at[j, pl.ds(0, 4 * ROWS)], send3.at[j])
        await_bytes(theirs.at[j], send5.at[j])

        @pl.when(j < near_until)
        def _():
            await_bytes(tile(j, 0), send4.at[j])
            await_bytes(tile(j, 0), send7.at[j])

        @pl.when(j >= near_until)
        def _():
            await_bytes(gathered.at[j, pl.ds(0, 2 * ROWS)], send4.at[j])

        @pl.when(j < direct_from)
        def _():
            await_bytes(shares.at[j, pl.ds(0, 6 * ROWS)], send6.at[j])
            await_bytes(shares.at[j, pl.ds(0, ROWS)], send8.at[j])

            @pl.when(core != j % 2)
            def _():
                await_bytes(shares.at[j, pl.ds(0, ROWS)], send8.at[j])

        @pl.when(j >= direct_from)
        def _():
            await_bytes(shares.at[j, pl.ds(0, (blocks - 1) * ROWS)], send6.at[j])

            @pl.when(core != j % 2)
            def _():
                await_bytes(shares.at[j, pl.ds(0, ROWS)], send6.at[j])

        @pl.when(j < chunks // 2)
        def _():
            await_bytes(result.at[tiles(0)], out_sem.at[j])


def body(gate_pre, up_pre, down_weight):
    rows, ff_dev = gate_pre.shape
    width = down_weight.shape[1]
    groups, blocks = lax.axis_size("tensor"), lax.axis_size("dp")
    chunks = rows // ROWS
    half = width // 2
    near_until = direct_from = chunks - 2
    order = ff_dev * groups
    table = jnp.asarray(sylvester(INNER), jnp.bfloat16)
    bf16 = jnp.bfloat16
    dma = pltpu.SemaphoreType.DMA
    return pl.pallas_call(
        functools.partial(kernel, 1.0 / order**0.5, near_until, direct_from),
        out_shape=jax.ShapeDtypeStruct((rows * blocks // groups, width), bf16),
        in_specs=[pl.BlockSpec(memory_space=pl.ANY)] * 3 + [pl.BlockSpec(memory_space=pltpu.VMEM)],
        out_specs=pl.BlockSpec(memory_space=pl.ANY),
        scratch_shapes=[
            pltpu.VMEM((chunks, ROWS, ff_dev), bf16),
            pltpu.VMEM((chunks, ROWS, ff_dev), bf16),
            pltpu.VMEM((ff_dev, width), bf16),
            pltpu.VMEM((ff_dev // INNER * ROWS, INNER), jnp.float32),
            pltpu.VMEM((chunks, ROWS, ff_dev), bf16),
            pltpu.VMEM((chunks * groups, ROWS, INNER), bf16),
            pltpu.VMEM((chunks * groups, ROWS, INNER), bf16),
            pltpu.VMEM((chunks, blocks * ROWS, ff_dev), bf16),
            pltpu.VMEM((chunks, blocks * ROWS, half), bf16),
            pltpu.VMEM((blocks * ROWS, half), jnp.float32),
            pltpu.VMEM((chunks, blocks * ROWS, half), bf16),
            pltpu.VMEM((chunks, blocks * ROWS, half), bf16),
            pltpu.VMEM(((chunks - direct_from) // 2, blocks * ROWS, width), bf16),
            pltpu.VMEM((direct_from, blocks * ROWS, half), bf16),
            pltpu.VMEM((direct_from, 2 * ROWS, half), bf16),
            pltpu.VMEM((direct_from // 2, 2 * ROWS, width), bf16),
            pltpu.VMEM((chunks // 2 * ROWS, width), bf16),
            dma((chunks,)),
            dma,
            dma((chunks // 2,)),
        ]
        + [dma((chunks,))] * 20,
        compiler_params=pltpu.CompilerParams(
            collective_id=0, has_side_effects=True, vmem_limit_bytes=56 * 2**20
        ),
        cost_estimate=pl.CostEstimate(
            flops=2 * rows * blocks * ff_dev * width,
            bytes_accessed=2 * ff_dev * width + 4 * rows * ff_dev,
            transcendentals=rows * ff_dev,
        ),
    )(gate_pre, up_pre, down_weight, table)


def solution(mesh):
    placed = (P("dp", "tensor"), P("dp", "tensor"), P("tensor", "dp"))
    return jax.shard_map(
        body, mesh=mesh, in_specs=placed, out_specs=P("tensor", "dp"), check_vma=False
    )
```

```python
import functools

import jax
import jax.numpy as jnp
import numpy as np
from jax import lax
from jax.experimental import pallas as pl
from jax.experimental.pallas import tpu as pltpu
from jax.sharding import PartitionSpec as P

MESH = pl.DeviceIdType.MESH
INNER = 256
ROWS = 16


def sylvester(order):
    table = np.ones((1, 1), np.float32)
    while table.shape[0] < order:
        table = np.block([[table, table], [table, -table]])
    return table


def butterfly(parts):
    half = 1
    while half < len(parts):
        for i in range(len(parts)):
            if i // half % 2 == 0:
                first, second = parts[i], parts[i + half]
                parts[i], parts[i + half] = first + second, first - second
        half = half * 2
    return parts


def kernel(
    scale, near_until, direct_from, gate_hbm, up_hbm, weight_hbm, table_hbm, out_ref,
    gate, up, weight, table, mixed, local, arrived, rotated, gathered, theirs, ours, swapped, shares, landed, over_y, sums, over_z, result,
    load_sem, weight_sem, table_sem, out_sem, send1, recv1, send2, recv2_own, recv2_near, send3, up3_own, up3_near, down3_own, down3_near,
    send4, recv4, send5, recv5, send6, recv6, send7, recv7, send8, recv8,
):
    dp, tensor = lax.axis_index("dp"), lax.axis_index("tensor")
    groups, blocks = lax.axis_size("tensor"), lax.axis_size("dp")
    chunks = gate.shape[0]
    half = weight.shape[1] // 2
    width = gate.shape[2]
    core, chip = tensor % 2, tensor // 2
    row, high = chip // 2, chip % 2
    near = dp + 1 - 2 * (dp % 2)
    ahead, behind, opposite = (dp + 2) % blocks, (dp + blocks - 2) % blocks, (dp + 4) % blocks
    peers = [(tensor + i) % groups for i in range(groups)]

    def remote(src, dst, send, recv, device):
        pltpu.make_async_remote_copy(
            src_ref=src, dst_ref=dst, send_sem=send, recv_sem=recv, device_id=device, device_id_type=MESH
        ).start()

    def await_bytes(like, sem):
        pltpu.make_async_copy(like, like, sem).wait()

    def tiles(i, n=1):
        return pl.ds(pl.multiple_of(i * ROWS, ROWS), n * ROWS)

    def first_row(j):
        return pl.multiple_of(j % 2 * (chunks // 2 * ROWS) + j // 2 * ROWS, ROWS)

    barrier = pltpu.get_barrier_semaphore()
    met = [(dp, p) for p in peers[1:]] + [(near, tensor), (ahead, tensor), (behind, tensor)]
    for device in met:
        pl.semaphore_signal(barrier, inc=1, device_id=device, device_id_type=MESH)

    pltpu.make_async_copy(table_hbm, table, table_sem).start()
    for j in range(chunks):
        rows = pl.ds(first_row(j), ROWS)
        pltpu.make_async_copy(gate_hbm.at[rows], gate.at[j], load_sem.at[j]).start()
        pltpu.make_async_copy(up_hbm.at[rows], up.at[j], load_sem.at[j]).start()
    pltpu.make_async_copy(weight_hbm, weight, weight_sem).start()

    def rotate_local(j):
        await_bytes(gate.at[pl.ds(0, 2)], load_sem.at[j])
        hidden = []
        for a in range(width // INNER):
            cols = pl.ds(a * INNER, INNER)
            v = gate[j, :, cols].astype(jnp.float32)
            u = up[j, :, cols].astype(jnp.float32)
            hidden.append((v / (1.0 + jnp.exp(-v)) * u).astype(jnp.bfloat16))
        mixed[...] = jnp.dot(
            jnp.concatenate(hidden, axis=0), table[...], preferred_element_type=jnp.float32
        )
        for lane in range(0, INNER, 128):
            parts = [mixed[pl.ds(a * ROWS, ROWS), pl.ds(lane, 128)] for a in range(len(hidden))]
            for a, part in enumerate(butterfly(parts)):
                local[j, :, pl.ds(a * INNER + lane, 128)] = part.astype(jnp.bfloat16)

    def piece(i):
        return pl.ds(pl.multiple_of(i * INNER, INNER), INNER)

    def send_local(j):
        slot = arrived.at[j * groups + tensor]
        pltpu.make_async_copy(local.at[j, :, piece(tensor)], slot, recv1.at[j]).start()
        for p in peers[1:]:
            remote(local.at[j, :, piece(p)], slot, send1.at[j], recv1.at[j], (dp, p))

    def rotate_groups(j):
        await_bytes(arrived.at[pl.ds(j * groups, groups)], recv1.at[j])
        for lane in range(0, INNER, 128):
            lanes = pl.ds(lane, 128)
            parts = [arrived[j * groups + g, :, lanes].astype(jnp.float32) for g in range(groups)]
            for g, part in enumerate(butterfly(parts)):
                rotated[j * groups + g, :, lanes] = (part * scale).astype(jnp.bfloat16)
        here = gathered.at[j, tiles(dp), piece(tensor)]
        pltpu.make_async_copy(rotated.at[j * groups + tensor], here, recv2_own.at[j]).start()
        for p in peers[1:]:
            remote(rotated.at[j * groups + p], here, send2.at[j], recv2_own.at[j], (dp, p))
        for p in peers:
            remote(rotated.at[j * groups + p], here, send2.at[j], recv2_near.at[j], (near, p))

    def tile(j, block):
        return gathered.at[j, tiles(block)]

    def left(j, block):
        return gathered.at[j, tiles(block), pl.ds(0, width // 2)]

    def right(j, block):
        return gathered.at[j, tiles(block), pl.ds(width // 2, width // 2)]

    def plane(block):
        return block + 1 - 2 * (dp % 2)

    def send_own(j):
        own = tile(j, dp)
        await_bytes(own, recv2_own.at[j])
        remote(own, own, send3.at[j], up3_own.at[j], (ahead, tensor))

        @pl.when(j < near_until)
        def _():
            remote(own, own, send3.at[j], down3_own.at[j], (behind, tensor))

    def send_other(j):
        own, other = tile(j, dp), tile(j, near)
        await_bytes(other, recv2_near.at[j])
        remote(other, other, send3.at[j], down3_near.at[j], (behind, tensor))
        remote(other, other, send3.at[j], up3_near.at[j], (ahead, tensor))

        @pl.when(j >= near_until)
        def _():
            remote(own, own, send3.at[j], down3_own.at[j], (behind, tensor))

    def forward(j):
        await_bytes(tile(j, behind), up3_own.at[j])

        @pl.when(j < near_until)
        def _():
            first, second = left(j, behind), right(j, ahead)
            remote(first, first, send4.at[j], recv4.at[j], (ahead, tensor))
            await_bytes(tile(j, ahead), down3_own.at[j])
            remote(second, second, send4.at[j], recv4.at[j], (behind, tensor))

        @pl.when(j >= near_until)
        def _():
            first, second = tile(j, behind), tile(j, plane(ahead))
            remote(first, first, send4.at[j], recv4.at[j], (ahead, tensor))
            await_bytes(second, down3_near.at[j])
            remote(second, second, send4.at[j], recv4.at[j], (behind, tensor))

    def across(j):
        far = tile(j, opposite)
        await_bytes(far, recv4.at[j])
        remote(far, far, send7.at[j], recv7.at[j], (near, tensor))

    mine = pl.ds(pl.multiple_of(core * half, half), half)

    def project(j):
        await_bytes(tile(j, plane(behind)), up3_near.at[j])

        @pl.when(j < near_until)
        def _():
            await_bytes(tile(j, plane(ahead)), down3_near.at[j])
            await_bytes(tile(j, plane(opposite)), recv7.at[j])

        @pl.when(j >= near_until)
        def _():
            await_bytes(tile(j, ahead), down3_own.at[j])
            await_bytes(gathered.at[j, pl.ds(0, 2 * ROWS)], recv4.at[j])

        cols = pl.ds(pl.multiple_of((1 - core) * half, half), half)
        term = jnp.dot(gathered[j], weight[:, cols], preferred_element_type=jnp.float32)
        theirs[j] = term.astype(jnp.bfloat16)

        remote(theirs.at[j], swapped.at[j], send5.at[j], recv5.at[j], (dp, tensor + 1 - 2 * core))
        ours[j % 2] = jnp.dot(gathered[j], weight[:, mine], preferred_element_type=jnp.float32)

    def deliver(j, share, there, send, recv, owner):
        @pl.when(core == j % 2)
        def _():
            pltpu.make_async_copy(share, there, recv).start()

        @pl.when(core != j % 2)
        def _():
            remote(share, there, send, recv, (dp, owner))

    def scatter(j):
        await_bytes(swapped.at[j], recv5.at[j])
        for block in range(blocks):
            rows = pl.ds(block * ROWS, ROWS)
            shares[j, rows, :] = (ours[j % 2, rows, :] + swapped[j, rows, :].astype(jnp.float32)).astype(jnp.bfloat16)

        @pl.when(j < direct_from)
        def _():
            slot = over_y.at[j, tiles(2 * row, 2)]
            own = shares.at[j, tiles(2 * row, 2)]
            pltpu.make_async_copy(own, slot, recv6.at[j]).start()
            for i in range(1, 4):
                to = (row + i) % 4
                part = shares.at[j, tiles(2 * to, 2)]
                remote(part, slot, send6.at[j], recv6.at[j], (dp, to * 4 + high * 2 + core))

        @pl.when(j >= direct_from)
        def _():
            there = landed.at[j // 2 - direct_from // 2, tiles(chip), mine]
            deliver(j, shares.at[j, tiles(chip)], there, send6.at[j], recv6.at[j], chip * 2 + j % 2)
            for i in range(1, blocks):
                to = (chip + i) % blocks
                share = shares.at[j, tiles(to)]
                remote(share, there, send6.at[j], recv6.at[j], (dp, to * 2 + j % 2))

    def scatter_z(j):
        await_bytes(over_y.at[j], recv6.at[j])
        for part in range(2):
            total = over_y[j, pl.ds(part * ROWS, ROWS), :].astype(jnp.float32)
            for i in range(1, 4):
                total = total + over_y[j, pl.ds((2 * i + part) * ROWS, ROWS), :].astype(jnp.float32)
            sums[j, pl.ds(part * ROWS, ROWS), :] = total.astype(jnp.bfloat16)
        there = over_z.at[j // 2, tiles(high), mine]
        other = row * 4 + (1 - high) * 2 + j % 2
        remote(sums.at[j, tiles(1 - high)], there, send8.at[j], recv8.at[j], (dp, other))
        deliver(j, sums.at[j, tiles(high)], there, send8.at[j], recv8.at[j], chip * 2 + j % 2)

    def finish(j):
        rows = tiles(j // 2)

        def add(source, count):
            for lane in range(0, 2 * half, 512):
                lanes = pl.ds(lane, 512)
                total = source[pl.ds(0, ROWS), lanes].astype(jnp.float32)
                for i in range(1, count):
                    total = total + source[pl.ds(i * ROWS, ROWS), lanes].astype(jnp.float32)
                result[rows, lanes] = total.astype(jnp.bfloat16)

        @pl.when(j < direct_from)
        def _():
            await_bytes(over_z.at[j // 2], recv8.at[j])
            add(over_z.at[j // 2], 2)

        @pl.when(j >= direct_from)
        def _():
            await_bytes(landed.at[j // 2 - direct_from // 2], recv6.at[j])
            add(landed.at[j // 2 - direct_from // 2], blocks)

        pltpu.make_async_copy(result.at[rows], out_ref.at[rows], out_sem.at[j // 2]).start()

    pltpu.make_async_copy(table_hbm, table, table_sem).wait()
    rotate_local(0)
    pl.semaphore_wait(barrier, len(met))

    send_local(0)
    rotate_local(1)
    send_local(1)

    @pl.loop(1, chunks + 8)
    def _(s):
        def stage(offset, step, first=0, last=chunks):
            @pl.when((s >= first + offset) & (s < last + offset))
            def _():
                step(s - offset)

        stage(1, rotate_groups)
        stage(-1, rotate_local, 2)
        stage(-1, send_local, 2)
        stage(2, send_own)
        stage(3, forward)
        stage(2, send_other)
        stage(4, across, 0, near_until)
        stage(6, scatter, 0, near_until)
        stage(5, scatter, near_until)
        stage(7, scatter_z, 0, direct_from)
        @pl.when(s == 5)
        def _():
            pltpu.make_async_copy(weight_hbm, weight, weight_sem).wait()

        stage(5, project, 0, near_until)
        stage(4, project, near_until)
        @pl.when((s >= 8) & (s % 2 == core))
        def _():
            finish(s - 8)

    @pl.loop(0, chunks)
    def _(j):
        await_bytes(arrived.at[pl.ds(0, groups - 1)], send1.at[j])
        await_bytes(rotated.at[pl.ds(0, 2 * groups - 1)], send2.at[j])
        await_bytes(gathered.at[j, pl.ds(0, 4 * ROWS)], send3.at[j])
        await_bytes(theirs.at[j], send5.at[j])

        @pl.when(j < near_until)
        def _():
            await_bytes(tile(j, 0), send4.at[j])
            await_bytes(tile(j, 0), send7.at[j])

        @pl.when(j >= near_until)
        def _():
            await_bytes(gathered.at[j, pl.ds(0, 2 * ROWS)], send4.at[j])

        @pl.when(j < direct_from)
        def _():
            await_bytes(shares.at[j, pl.ds(0, 6 * ROWS)], send6.at[j])
            await_bytes(shares.at[j, pl.ds(0, ROWS)], send8.at[j])

            @pl.when(core != j % 2)
            def _():
                await_bytes(shares.at[j, pl.ds(0, ROWS)], send8.at[j])

        @pl.when(j >= direct_from)
        def _():
            await_bytes(shares.at[j, pl.ds(0, (blocks - 1) * ROWS)], send6.at[j])

            @pl.when(core != j % 2)
            def _():
                await_bytes(shares.at[j, pl.ds(0, ROWS)], send6.at[j])

        @pl.when(j < chunks // 2)
        def _():
            await_bytes(result.at[tiles(0)], out_sem.at[j])


def body(gate_pre, up_pre, down_weight):
    rows, ff_dev = gate_pre.shape
    width = down_weight.shape[1]
    groups, blocks = lax.axis_size("tensor"), lax.axis_size("dp")
    chunks = rows // ROWS
    half = width // 2
    near_until, direct_from = 6, 6
    order = ff_dev * groups
    table = jnp.asarray(sylvester(INNER), jnp.bfloat16)
    bf16 = jnp.bfloat16
    dma = pltpu.SemaphoreType.DMA
    return pl.pallas_call(
        functools.partial(kernel, 1.0 / order**0.5, near_until, direct_from),
        out_shape=jax.ShapeDtypeStruct((rows * blocks // groups, width), bf16),
        in_specs=[pl.BlockSpec(memory_space=pl.ANY)] * 4,
        out_specs=pl.BlockSpec(memory_space=pl.ANY),
        scratch_shapes=[
            pltpu.VMEM((chunks, ROWS, ff_dev), bf16),
            pltpu.VMEM((chunks, ROWS, ff_dev), bf16),
            pltpu.VMEM((ff_dev, width), bf16),
            pltpu.VMEM((INNER, INNER), bf16),
            pltpu.VMEM((ff_dev // INNER * ROWS, INNER), jnp.float32),
            pltpu.VMEM((chunks, ROWS, ff_dev), bf16),
            pltpu.VMEM((chunks * groups, ROWS, INNER), bf16),
            pltpu.VMEM((chunks * groups, ROWS, INNER), bf16),
            pltpu.VMEM((chunks, blocks * ROWS, ff_dev), bf16),
            pltpu.VMEM((chunks, blocks * ROWS, half), bf16),
            pltpu.VMEM((2, blocks * ROWS, half), jnp.float32),
            pltpu.VMEM((chunks, blocks * ROWS, half), bf16),
            pltpu.VMEM((chunks, blocks * ROWS, half), bf16),
            pltpu.VMEM(((chunks - direct_from) // 2, blocks * ROWS, width), bf16),
            pltpu.VMEM((direct_from, blocks * ROWS, half), bf16),
            pltpu.VMEM((direct_from, 2 * ROWS, half), bf16),
            pltpu.VMEM((direct_from // 2, 2 * ROWS, width), bf16),
            pltpu.VMEM((chunks // 2 * ROWS, width), bf16),
            dma((chunks,)),
            dma,
            dma,
            dma((chunks // 2,)),
        ]
        + [dma((chunks,))] * 20,
        compiler_params=pltpu.CompilerParams(
            collective_id=0, has_side_effects=True, vmem_limit_bytes=56 * 2**20
        ),
        cost_estimate=pl.CostEstimate(
            flops=2 * rows * blocks * ff_dev * width,
            bytes_accessed=2 * ff_dev * width + 4 * rows * ff_dev,
            transcendentals=rows * ff_dev,
        ),
    )(gate_pre, up_pre, down_weight, table)


def solution(mesh):
    placed = (P("dp", "tensor"), P("dp", "tensor"), P("tensor", "dp"))
    return jax.shard_map(
        body, mesh=mesh, in_specs=placed, out_specs=P("tensor", "dp"), check_vma=False
    )
```

```python
import functools

import jax
import jax.numpy as jnp
import numpy as np
from jax import lax
from jax.experimental import pallas as pl
from jax.experimental.pallas import tpu as pltpu
from jax.sharding import PartitionSpec as P

MESH = pl.DeviceIdType.MESH
INNER = 256
ROWS = 16


def sylvester(order):
    table = np.ones((1, 1), np.float32)
    while table.shape[0] < order:
        table = np.block([[table, table], [table, -table]])
    return table


def butterfly(parts):
    half = 1
    while half < len(parts):
        for i in range(len(parts)):
            if i // half % 2 == 0:
                first, second = parts[i], parts[i + half]
                parts[i], parts[i + half] = first + second, first - second
        half = half * 2
    return parts


def kernel(
    scale, near_until, direct_from, gate_hbm, up_hbm, weight_hbm, table_hbm, out_ref,
    gate, up, weight, table, mixed, local, arrived, rotated, gathered, theirs, ours, swapped, shares, landed, over_y, sums, over_z, result,
    load_sem, weight_sem, table_sem, out_sem, send1, recv1, send2, recv2_own, recv2_near, send3, up3_own, up3_near, down3_own, down3_near,
    send4, recv4, send5, recv5, send6, recv6, send7, recv7, send8, recv8,
):
    dp, tensor = lax.axis_index("dp"), lax.axis_index("tensor")
    groups, blocks = lax.axis_size("tensor"), lax.axis_size("dp")
    chunks = gate.shape[0]
    half = weight.shape[1] // 2
    width = gate.shape[2]
    core, chip = tensor % 2, tensor // 2
    row, high = chip // 2, chip % 2
    near = dp + 1 - 2 * (dp % 2)
    ahead, behind = (dp + 2) % blocks, (dp + blocks - 2) % blocks
    column, plane, last = dp // 2, dp % 2, chunks - 1
    peers = [(tensor + i) % groups for i in range(groups)]

    def remote(src, dst, send, recv, device):
        pltpu.make_async_remote_copy(
            src_ref=src, dst_ref=dst, send_sem=send, recv_sem=recv, device_id=device, device_id_type=MESH
        ).start()

    def await_bytes(like, sem):
        pltpu.make_async_copy(like, like, sem).wait()

    def tiles(i, n=1):
        return pl.ds(pl.multiple_of(i * ROWS, ROWS), n * ROWS)

    def first_row(j):
        return pl.multiple_of(j % 2 * (chunks // 2 * ROWS) + j // 2 * ROWS, ROWS)

    barrier = pltpu.get_barrier_semaphore()
    met = [(dp, p) for p in peers[1:]] + [(near, tensor), (ahead, tensor), (behind, tensor)]
    for device in met:
        pl.semaphore_signal(barrier, inc=1, device_id=device, device_id_type=MESH)

    pltpu.make_async_copy(table_hbm, table, table_sem).start()
    for j in range(chunks):
        rows = pl.ds(first_row(j), ROWS)
        pltpu.make_async_copy(gate_hbm.at[rows], gate.at[j], load_sem.at[j]).start()
        pltpu.make_async_copy(up_hbm.at[rows], up.at[j], load_sem.at[j]).start()
    pltpu.make_async_copy(weight_hbm, weight, weight_sem).start()

    def rotate_local(j):
        await_bytes(gate.at[pl.ds(0, 2)], load_sem.at[j])
        hidden = []
        for a in range(width // INNER):
            cols = pl.ds(a * INNER, INNER)
            v = gate[j, :, cols].astype(jnp.float32)
            u = up[j, :, cols].astype(jnp.float32)
            hidden.append((v / (1.0 + jnp.exp(-v)) * u).astype(jnp.bfloat16))
        mixed[...] = jnp.dot(
            jnp.concatenate(hidden, axis=0), table[...], preferred_element_type=jnp.float32
        )
        for lane in range(0, INNER, 128):
            parts = [mixed[pl.ds(a * ROWS, ROWS), pl.ds(lane, 128)] for a in range(len(hidden))]
            for a, part in enumerate(butterfly(parts)):
                local[j, :, pl.ds(a * INNER + lane, 128)] = part.astype(jnp.bfloat16)

    def piece(i):
        return pl.ds(pl.multiple_of(i * INNER, INNER), INNER)

    def send_local(j):
        slot = arrived.at[j * groups + tensor]
        pltpu.make_async_copy(local.at[j, :, piece(tensor)], slot, recv1.at[j]).start()
        for p in peers[1:]:
            remote(local.at[j, :, piece(p)], slot, send1.at[j], recv1.at[j], (dp, p))

    def rotate_groups(j):
        await_bytes(arrived.at[pl.ds(j * groups, groups)], recv1.at[j])
        for lane in range(0, INNER, 128):
            lanes = pl.ds(lane, 128)
            parts = [arrived[j * groups + g, :, lanes].astype(jnp.float32) for g in range(groups)]
            for g, part in enumerate(butterfly(parts)):
                rotated[j * groups + g, :, lanes] = (part * scale).astype(jnp.bfloat16)
        here = gathered.at[j, tiles(2 + plane), piece(tensor)]
        pltpu.make_async_copy(rotated.at[j * groups + tensor], here, recv2_own.at[j]).start()
        for p in peers[1:]:
            remote(rotated.at[j * groups + p], here, send2.at[j], recv2_own.at[j], (dp, p))
        for p in peers:
            remote(rotated.at[j * groups + p], here, send2.at[j], recv2_near.at[j], (near, p))

    def tile(j, block):
        return gathered.at[j, tiles(block)]

    def left(j, block):
        return gathered.at[j, tiles(block), pl.ds(0, width // 2)]

    def right(j, block):
        return gathered.at[j, tiles(block), pl.ds(width // 2, width // 2)]

    def send_own(j):
        own = tile(j, 2 + plane)
        await_bytes(own, recv2_own.at[j])
        remote(own, tile(j, plane), send3.at[j], up3_own.at[j], (ahead, tensor))

        @pl.when(j < near_until)
        def _():
            remote(own, tile(j, 4 + plane), send3.at[j], down3_own.at[j], (behind, tensor))

    def send_other(j):
        own, other = tile(j, 2 + plane), tile(j, 3 - plane)
        await_bytes(other, recv2_near.at[j])
        remote(other, tile(j, 5 - plane), send3.at[j], down3_near.at[j], (behind, tensor))
        remote(other, tile(j, 1 - plane), send3.at[j], up3_near.at[j], (ahead, tensor))

        @pl.when(j >= near_until)
        def _():
            remote(own, tile(j, 4 + plane), send3.at[j], down3_own.at[j], (behind, tensor))

    def forward(j):
        await_bytes(tile(j, plane), up3_own.at[j])

        @pl.when(j < near_until)
        def _():
            remote(left(j, plane), left(j, 6 + plane), send4.at[j], recv4.at[j], (ahead, tensor))
            await_bytes(tile(j, 4 + plane), down3_own.at[j])
            remote(right(j, 4 + plane), right(j, 6 + plane), send4.at[j], recv4.at[j], (behind, tensor))

        @pl.when(j >= near_until)
        def _():
            remote(tile(j, plane), tile(j, 6 + plane), send4.at[j], recv4.at[j], (ahead, tensor))
            await_bytes(tile(j, 5 - plane), down3_near.at[j])
            remote(tile(j, 5 - plane), tile(j, 7 - plane), send4.at[j], recv4.at[j], (behind, tensor))

    def across(j):
        far = tile(j, 6 + plane)
        await_bytes(far, recv4.at[j])
        remote(far, far, send7.at[j], recv7.at[j], (near, tensor))

    mine = pl.ds(pl.multiple_of(core * half, half), half)

    def multiply(j, first, count, send, recv):
        rows = pl.ds(first * ROWS, count * ROWS)
        other = pl.ds(pl.multiple_of((1 - core) * half, half), half)
        term = jnp.dot(gathered[j, rows], weight[:, other], preferred_element_type=jnp.float32)
        theirs[j, rows] = term.astype(jnp.bfloat16)
        remote(theirs.at[j, rows], swapped.at[j, rows], send.at[j], recv.at[j], (dp, tensor + 1 - 2 * core))
        ours[j % 3, rows] = jnp.dot(gathered[j, rows], weight[:, mine], preferred_element_type=jnp.float32)

    def project(j):
        await_bytes(tile(j, 1 - plane), up3_near.at[j])

        @pl.when(j < near_until)
        def _():
            await_bytes(tile(j, 5 - plane), down3_near.at[j])
            await_bytes(tile(j, 7 - plane), recv7.at[j])

        @pl.when(j >= near_until)
        def _():
            await_bytes(tile(j, 4 + plane), down3_own.at[j])
            await_bytes(gathered.at[j, tiles(6, 2)], recv4.at[j])

        multiply(j, 0, blocks, send5, recv5)

    def project_early(j):
        await_bytes(tile(j, 1 - plane), up3_near.at[j])
        await_bytes(tile(j, 4 + plane), down3_own.at[j])
        multiply(j, 0, blocks - 2, send5, recv5)

    def project_late(j):
        await_bytes(gathered.at[j, tiles(6, 2)], recv4.at[j])
        multiply(j, blocks - 2, 2, send7, recv7)

    def slot(y):
        return (y + 5 - column) % 4

    def add_shares(j, first, count):
        for block in range(first, first + count):
            rows = pl.ds(block * ROWS, ROWS)
            shares[j, rows, :] = (ours[j % 3, rows, :] + swapped[j, rows, :].astype(jnp.float32)).astype(jnp.bfloat16)

    def landing(j):
        return landed.at[j // 2 - direct_from // 2, tiles(chip), mine]

    def scatter_part(j, first, count, recv):
        await_bytes(swapped.at[j, pl.ds(first * ROWS, count * ROWS)], recv.at[j])
        add_shares(j, first, count)
        for block in range(first, first + count):
            owner = ((column + block // 2 + 3) % 4 * 2 + block % 2) * 2 + j % 2
            share = shares.at[j, pl.ds(block * ROWS, ROWS)]

            @pl.when(owner == tensor)
            def _():
                pltpu.make_async_copy(share, landing(j), recv6.at[j]).start()

            @pl.when(owner != tensor)
            def _():
                remote(share, landing(j), send6.at[j], recv6.at[j], (dp, owner))

    def scatter_early(j):
        scatter_part(j, 0, blocks - 2, recv5)

    def scatter_late(j):
        scatter_part(j, blocks - 2, 2, recv7)

    def deliver(j, share, there, send, recv, owner):
        @pl.when(core == j % 2)
        def _():
            pltpu.make_async_copy(share, there, recv).start()

        @pl.when(core != j % 2)
        def _():
            remote(share, there, send, recv, (dp, owner))

    def scatter(j):
        await_bytes(swapped.at[j], recv5.at[j])
        add_shares(j, 0, blocks)

        @pl.when(j < direct_from)
        def _():
            there = over_y.at[j, tiles(2 * row, 2)]
            own = shares.at[j, tiles(2 * slot(row), 2)]
            pltpu.make_async_copy(own, there, recv6.at[j]).start()
            for i in range(1, 4):
                to = (row + i) % 4
                part = shares.at[j, tiles(2 * slot(to), 2)]
                remote(part, there, send6.at[j], recv6.at[j], (dp, to * 4 + high * 2 + core))

        @pl.when(j >= direct_from)
        def _():
            there = landing(j)
            own = shares.at[j, tiles(2 * slot(row) + high)]
            deliver(j, own, there, send6.at[j], recv6.at[j], chip * 2 + j % 2)
            for i in range(1, blocks):
                to = (chip + i) % blocks
                share = shares.at[j, tiles(2 * slot(to // 2) + to % 2)]
                remote(share, there, send6.at[j], recv6.at[j], (dp, to * 2 + j % 2))

    def scatter_z(j):
        await_bytes(over_y.at[j], recv6.at[j])
        for part in range(2):
            total = over_y[j, pl.ds(part * ROWS, ROWS), :].astype(jnp.float32)
            for i in range(1, 4):
                total = total + over_y[j, pl.ds((2 * i + part) * ROWS, ROWS), :].astype(jnp.float32)
            sums[j, pl.ds(part * ROWS, ROWS), :] = total.astype(jnp.bfloat16)
        there = over_z.at[j // 2, tiles(high), mine]
        other = row * 4 + (1 - high) * 2 + j % 2
        remote(sums.at[j, tiles(1 - high)], there, send8.at[j], recv8.at[j], (dp, other))
        deliver(j, sums.at[j, tiles(high)], there, send8.at[j], recv8.at[j], chip * 2 + j % 2)

    def finish(j):
        rows = tiles(j // 2)

        def add(source, count):
            for lane in range(0, 2 * half, 512):
                lanes = pl.ds(lane, 512)
                total = source[pl.ds(0, ROWS), lanes].astype(jnp.float32)
                for i in range(1, count):
                    total = total + source[pl.ds(i * ROWS, ROWS), lanes].astype(jnp.float32)
                result[rows, lanes] = total.astype(jnp.bfloat16)

        @pl.when(j < direct_from)
        def _():
            await_bytes(over_z.at[j // 2], recv8.at[j])
            add(over_z.at[j // 2], 2)

        @pl.when(j >= direct_from)
        def _():
            await_bytes(landed.at[j // 2 - direct_from // 2], recv6.at[j])
            add(landed.at[j // 2 - direct_from // 2], blocks)

        pltpu.make_async_copy(result.at[rows], out_ref.at[rows], out_sem.at[j // 2]).start()

    pltpu.make_async_copy(table_hbm, table, table_sem).wait()
    rotate_local(0)
    pl.semaphore_wait(barrier, len(met))

    send_local(0)
    rotate_local(1)
    send_local(1)

    @pl.loop(1, chunks + 9)
    def _(s):
        def stage(offset, step, first=0, end=chunks):
            @pl.when((s >= first + offset) & (s < end + offset))
            def _():
                step(s - offset)

        stage(1, rotate_groups)
        stage(-1, rotate_local, 2)
        stage(-1, send_local, 2)
        stage(2, send_own)
        stage(4, forward)
        stage(2, send_other)
        stage(5, across, 0, near_until)
        stage(7, scatter, 0, near_until - 1)
        stage(8, scatter_z, 0, direct_from)

        @pl.when(s == 6)
        def _():
            pltpu.make_async_copy(weight_hbm, weight, weight_sem).wait()

        stage(6, project, 0, near_until)
        stage(5, project, near_until, last)
        stage(6, scatter, near_until - 1, near_until)
        stage(5, scatter, near_until, last)
        stage(4, project_early, last)
        stage(4, scatter_early, last)
        stage(5, project_late, last)
        stage(5, scatter_late, last)

        @pl.when((s >= 9) & ((s - 9) % 2 == core))
        def _():
            finish(s - 9)

    @pl.loop(0, chunks)
    def _(j):
        await_bytes(arrived.at[pl.ds(0, groups - 1)], send1.at[j])
        await_bytes(rotated.at[pl.ds(0, 2 * groups - 1)], send2.at[j])
        await_bytes(gathered.at[j, pl.ds(0, 4 * ROWS)], send3.at[j])

        @pl.when(j < last)
        def _():
            await_bytes(theirs.at[j], send5.at[j])

        @pl.when(j == last)
        def _():
            await_bytes(theirs.at[j, pl.ds(0, 6 * ROWS)], send5.at[j])
            await_bytes(theirs.at[j, pl.ds(0, 2 * ROWS)], send7.at[j])

        @pl.when(j < near_until)
        def _():
            await_bytes(tile(j, 0), send4.at[j])
            await_bytes(tile(j, 0), send7.at[j])

        @pl.when(j >= near_until)
        def _():
            await_bytes(gathered.at[j, pl.ds(0, 2 * ROWS)], send4.at[j])

        @pl.when(j < direct_from)
        def _():
            await_bytes(shares.at[j, pl.ds(0, 6 * ROWS)], send6.at[j])
            await_bytes(shares.at[j, pl.ds(0, ROWS)], send8.at[j])

            @pl.when(core != j % 2)
            def _():
                await_bytes(shares.at[j, pl.ds(0, ROWS)], send8.at[j])

        @pl.when(j >= direct_from)
        def _():
            await_bytes(shares.at[j, pl.ds(0, (blocks - 1) * ROWS)], send6.at[j])

            @pl.when(core != j % 2)
            def _():
                await_bytes(shares.at[j, pl.ds(0, ROWS)], send6.at[j])

        @pl.when(j < chunks // 2)
        def _():
            await_bytes(result.at[tiles(0)], out_sem.at[j])


def body(gate_pre, up_pre, down_weight):
    rows, ff_dev = gate_pre.shape
    width = down_weight.shape[1]
    groups, blocks = lax.axis_size("tensor"), lax.axis_size("dp")
    chunks = rows // ROWS
    half = width // 2
    near_until, direct_from = chunks - 2, chunks - 4
    order = ff_dev * groups
    table = jnp.asarray(sylvester(INNER), jnp.bfloat16)
    bf16 = jnp.bfloat16
    dma = pltpu.SemaphoreType.DMA
    return pl.pallas_call(
        functools.partial(kernel, 1.0 / order**0.5, near_until, direct_from),
        out_shape=jax.ShapeDtypeStruct((rows * blocks // groups, width), bf16),
        in_specs=[pl.BlockSpec(memory_space=pl.ANY)] * 4,
        out_specs=pl.BlockSpec(memory_space=pl.ANY),
        scratch_shapes=[
            pltpu.VMEM((chunks, ROWS, ff_dev), bf16),
            pltpu.VMEM((chunks, ROWS, ff_dev), bf16),
            pltpu.VMEM((ff_dev, width), bf16),
            pltpu.VMEM((INNER, INNER), bf16),
            pltpu.VMEM((ff_dev // INNER * ROWS, INNER), jnp.float32),
            pltpu.VMEM((chunks, ROWS, ff_dev), bf16),
            pltpu.VMEM((chunks * groups, ROWS, INNER), bf16),
            pltpu.VMEM((chunks * groups, ROWS, INNER), bf16),
            pltpu.VMEM((chunks, blocks * ROWS, ff_dev), bf16),
            pltpu.VMEM((chunks, blocks * ROWS, half), bf16),
            pltpu.VMEM((3, blocks * ROWS, half), jnp.float32),
            pltpu.VMEM((chunks, blocks * ROWS, half), bf16),
            pltpu.VMEM((chunks, blocks * ROWS, half), bf16),
            pltpu.VMEM(((chunks - direct_from) // 2, blocks * ROWS, width), bf16),
            pltpu.VMEM((direct_from, blocks * ROWS, half), bf16),
            pltpu.VMEM((direct_from, 2 * ROWS, half), bf16),
            pltpu.VMEM((direct_from // 2, 2 * ROWS, width), bf16),
            pltpu.VMEM((chunks // 2 * ROWS, width), bf16),
            dma((chunks,)),
            dma,
            dma,
            dma((chunks // 2,)),
        ]
        + [dma((chunks,))] * 20,
        compiler_params=pltpu.CompilerParams(
            collective_id=0, has_side_effects=True, vmem_limit_bytes=56 * 2**20
        ),
        cost_estimate=pl.CostEstimate(
            flops=2 * rows * blocks * ff_dev * width,
            bytes_accessed=2 * ff_dev * width + 4 * rows * ff_dev,
            transcendentals=rows * ff_dev,
        ),
    )(gate_pre, up_pre, down_weight, table)


def solution(mesh):
    placed = (P("dp", "tensor"), P("dp", "tensor"), P("tensor", "dp"))
    return jax.shard_map(
        body, mesh=mesh, in_specs=placed, out_specs=P("tensor", "dp"), check_vma=False
    )
```
